128 devices in a mesh: rep: 2 (over core), tp: 32 (over y_lo, z, x), att: 2 (over y_hi).
Axes of the slice: x: 4, y: 4 (y_hi: 2, y_lo: 2; y = y_hi * 2 + y_lo), z: 4, core: 2. Of those that a mesh axis runs over, the one named last changes fastest.
Arguments:
- inputs: bfloat16 [2, 128, 12288], P(None, ('rep', 'tp', 'att')), may hold values from -6 to 6
- cotangent: bfloat16 [2, 128, 12288], P(None, ('rep', 'tp', 'att')), may hold values from -1.5 to 1.5
- gate_weight: bfloat16 [14336, 12288], P(('tp', 'att')), may hold values from -0.0546875 to 0.0546875
- up_weight: bfloat16 [14336, 12288], P(('tp', 'att')), may hold values from -0.0546875 to 0.0546875
- down_weight: bfloat16 [14336, 12288], P(('tp', 'att')), may hold values from -0.046875 to 0.046875
Outputs:
- input_grad: bfloat16 [2, 128, 12288], P(None, ('rep', 'tp', 'att'))
- gate_grad: bfloat16 [14336, 12288], P(('tp', 'att'), 'rep')
- up_grad: bfloat16 [14336, 12288], P(('tp', 'att'), 'rep')
- down_grad: bfloat16 [14336, 12288], P(('tp', 'att'), 'rep')
The draws below stay inside these ranges and needn't reach their ends.
All inputs are finite; a program needn't handle non-finite values.
Results may differ from the reference program's by a relative error of at most 0.0054.
Values may be sent and summed in bfloat16 or wider, within the bound.
No kernel may reach another device: no remote copies, remote signals or barrier semaphores. Data moves between devices by JAX's collectives and lax.ppermute only.
A program may use at most 192 MiB of HBM per device.

```python
import jax
import jax.numpy as jnp
from jax import lax

D = 12288
FF = 14336
MICRO = 2
ROWS = 128


def block_levels(key, extent, pieces, smallest, largest):
    factor_of, own = 1.0, jax.random.fold_in(key, 6)
    for position, parts in pieces:
        draws = jnp.exp(jax.random.uniform(jax.random.fold_in(own, position), (parts,), jnp.float32, smallest / len(pieces), largest / len(pieces)))
        factor_of = factor_of * jnp.repeat(draws, extent[position] // parts).reshape([-1 if axis == position else 1 for axis in range(len(extent))])
    return factor_of


def bell_draw(stream_key, extent, scale, limit, split=(), held_as=jnp.bfloat16):
    values = jax.random.normal(stream_key, extent, jnp.float32) * scale
    if len(split) > 0:
        values = block_levels(stream_key, extent, split, -0.22, 0.18) * values
    return jnp.clip(values, min=-limit, max=limit).astype(held_as)


def setup_inputs(seed: int = 0) -> dict:
    splits = jax.random.split(jax.random.key(seed), 6)
    inputs = bell_draw(splits[0], (MICRO, ROWS, D), 1.0, 6.0, ((1, 128),))
    cotangent = bell_draw(splits[1], (MICRO, ROWS, D), 0.25, 1.5, ((1, 128),))
    gate_weight = bell_draw(splits[2], (FF, D), D ** -0.5, 0.0546875, ((0, 64),))
    up_weight = bell_draw(splits[3], (FF, D), D ** -0.5, 0.0546875, ((0, 64),))
    down_weight = bell_draw(splits[4], (FF, D), FF ** -0.5, 0.046875, ((0, 64),))
    return {"inputs": inputs, "cotangent": cotangent, "gate_weight": gate_weight, "up_weight": up_weight, "down_weight": down_weight}


def contract_last(left, right):
    return lax.dot_general(left, right, (((1,), (1,)), ((), ())), preferred_element_type=jnp.float32)


def contract_first(left, right):
    return lax.dot_general(left, right, (((0,), (0,)), ((), ())), preferred_element_type=jnp.float32)


def reference(inputs, cotangent, gate_weight, up_weight, down_weight):
    width = inputs.shape[2]
    grads = []
    gate_sum = jnp.zeros(gate_weight.shape, jnp.float32)
    up_sum = jnp.zeros(gate_weight.shape, jnp.float32)
    down_sum = jnp.zeros(gate_weight.shape, jnp.float32)
    for micro in range(MICRO):
        rows_in = inputs[micro]
        rows_cot = cotangent[micro]
        pre_gate = contract_last(rows_in, gate_weight)
        pre_up = contract_last(rows_in, up_weight)
        sig = jax.nn.sigmoid(pre_gate)
        act = pre_gate * sig
        hidden = (act * pre_up).astype(jnp.bfloat16)
        hidden_grad = contract_last(rows_cot, down_weight)
        gate_part = (hidden_grad * pre_up * sig * (1.0 + pre_gate * (1.0 - sig))).astype(jnp.bfloat16)
        up_part = (hidden_grad * act).astype(jnp.bfloat16)
        in_grad = jnp.dot(gate_part, gate_weight, preferred_element_type=jnp.float32)
        in_grad = in_grad + jnp.dot(up_part, up_weight, preferred_element_type=jnp.float32)
        grads.append(in_grad.astype(jnp.bfloat16))
        gate_sum = gate_sum + contract_first(gate_part, rows_in)
        up_sum = up_sum + contract_first(up_part, rows_in)
        down_sum = down_sum + contract_first(hidden, rows_cot)
    input_grad = jnp.stack(grads)
    return (input_grad, gate_sum.astype(jnp.bfloat16), up_sum.astype(jnp.bfloat16), down_sum.astype(jnp.bfloat16))
```

```python
import functools

import jax
import jax.numpy as jnp
import numpy as np
from jax import lax
from jax.experimental import pallas as pl
from jax.experimental.pallas import tpu as pltpu
from jax.sharding import PartitionSpec as P

AXES = ("rep", "tp", "att")
CHUNKS = (("x", "y", "z"), ("y", "z", "x"), ("z", "x", "y"))
GROUP = 32
VMEM_LIMIT = 56 * 1024 * 1024


def linear(core, x, y, z):
    return core * 64 + ((y % 2) * 16 + z * 4 + x) * 2 + y // 2


def pairs(moves, flip=0):
    result = []
    for core in range(2):
        dx, dy, dz = moves[core]
        for x in range(4):
            for y in range(4):
                for z in range(4):
                    result.append(
                        (linear(core, x, y, z), linear(core ^ flip, x ^ dx, y ^ dy, z ^ dz))
                    )
    return sorted(result)


def neighbour(axes, stage):
    moves = []
    for core in range(2):
        distance = 1 if core == stage else 3
        moves.append(tuple(distance if name in axes else 0 for name in "xyz"))
    return pairs(moves)


OTHER_CORE = pairs([(0, 0, 0)] * 2, flip=1)


def send(value, route):
    return lax.ppermute(value, AXES, route)


def label_order(axes):
    bit = {"x": 1, "y": 2, "z": 4}
    return [
        sum(bit[axis] for place, axis in enumerate(axes) if index >> place & 1)
        for index in range(8)
    ]


def forward_kernel(third, *refs):
    pieces, (gate_hbm, up_hbm, down_hbm), out_ref = refs[:24], refs[24:27], refs[27]
    rows_in, rows_cot, gate, up, down, sems, weight_sems = refs[28:]
    start = lax.axis_index("rep") * (3 * third)
    weight_copies = []
    for k in range(3):
        for i, (source, target) in enumerate(((gate_hbm, gate), (up_hbm, up), (down_hbm, down))):
            copy = pltpu.make_async_copy(
                source.at[:, pl.ds(pl.multiple_of(start + k * third, third), third)],
                target.at[:, pl.ds(k * third, third)],
                weight_sems.at[3 * k + i],
            )
            copy.start()
            weight_copies.append(copy)
    copies = []
    for k in range(3):
        for label in range(8):
            piece = pieces[8 * k + label]
            for i, target in enumerate((rows_in, rows_cot)):
                copy = pltpu.make_async_copy(
                    piece.at[i],
                    target.at[pl.ds(GROUP * label, GROUP), pl.ds(k * third, third)],
                    sems.at[16 * k + 2 * label + i],
                )
                copy.start()
                copies.append(copy)
    for k in range(3):
        columns = slice(k * third, (k + 1) * third)
        for copy in copies[16 * k : 16 * k + 16]:
            copy.wait()
        for i, (rows, weight) in enumerate(((rows_in, gate), (rows_in, up), (rows_cot, down))):
            weight_copies[3 * k + i].wait()
            product = lax.dot_general(
                rows[:, columns],
                weight[:, columns],
                (((1,), (1,)), ((), ())),
                preferred_element_type=jnp.float32,
            )
            if k == 0:
                out_ref[i] = product
            else:
                out_ref[i] += product


def forward(pieces, weights):
    local_ff, width = weights[0].shape
    half, third = width // 2, width // 6
    rows = 8 * GROUP
    any_spec = pl.BlockSpec(memory_space=pl.ANY)
    return pl.pallas_call(
        functools.partial(forward_kernel, third),
        out_shape=jax.ShapeDtypeStruct((3, rows, local_ff), jnp.float32),
        in_specs=[any_spec] * 27,
        out_specs=pl.BlockSpec(memory_space=pltpu.VMEM),
        scratch_shapes=[
            pltpu.VMEM((rows, half), jnp.bfloat16),
            pltpu.VMEM((rows, half), jnp.bfloat16),
            pltpu.VMEM((local_ff, half), jnp.bfloat16),
            pltpu.VMEM((local_ff, half), jnp.bfloat16),
            pltpu.VMEM((local_ff, half), jnp.bfloat16),
            pltpu.SemaphoreType.DMA((48,)),
            pltpu.SemaphoreType.DMA((9,)),
        ],
        compiler_params=pltpu.CompilerParams(vmem_limit_bytes=VMEM_LIMIT),
        cost_estimate=pl.CostEstimate(
            flops=6 * rows * local_ff * half, bytes_accessed=16 * 2**20, transcendentals=0
        ),
    )(*pieces, *weights)


def permuted(one_hot, value):
    high = value.astype(jnp.bfloat16)
    rest = value - high.astype(jnp.float32)
    middle = rest.astype(jnp.bfloat16)
    low = (rest - middle.astype(jnp.float32)).astype(jnp.bfloat16)
    return (
        jnp.dot(one_hot, high, preferred_element_type=jnp.float32)
        + jnp.dot(one_hot, middle, preferred_element_type=jnp.float32)
        + jnp.dot(one_hot, low, preferred_element_type=jnp.float32)
    )


def middle_kernel(third, *refs):
    part, other, one_hot, gate_hbm, up_hbm = refs[:5]
    sends, keeps, (gate_out, up_out, hidden_out) = refs[5:8], refs[8:11], refs[11:14]
    gate, up, weight_sems = refs[14:]
    start = lax.axis_index("rep") * (3 * third)
    copies = []
    for k in range(3):
        for i, (source, target) in enumerate(((gate_hbm, gate), (up_hbm, up))):
            copy = pltpu.make_async_copy(
                source.at[:, pl.ds(pl.multiple_of(start + k * third, third), third)],
                target.at[:, pl.ds(k * third, third)],
                weight_sems.at[2 * k + i],
            )
            copy.start()
            copies.append(copy)
    matrix = one_hot[...]
    pre_gate = part[0] + permuted(matrix, other[0])
    pre_up = part[1] + permuted(matrix, other[1])
    hidden_grad = part[2] + permuted(matrix, other[2])
    sig = jax.nn.sigmoid(pre_gate)
    act = pre_gate * sig
    hidden_out[...] = (act * pre_up).astype(jnp.bfloat16)
    gate_out[...] = (hidden_grad * pre_up * sig * (1.0 + pre_gate * (1.0 - sig))).astype(
        jnp.bfloat16
    )
    up_out[...] = (hidden_grad * act).astype(jnp.bfloat16)
    for k in range(3):
        columns = slice(k * third, (k + 1) * third)
        order = label_order(CHUNKS[k])
        copies[2 * k].wait()
        copies[2 * k + 1].wait()
        for first, target in ((4, sends[k]), (0, keeps[k])):
            picks = [slice(GROUP * b, GROUP * b + GROUP) for b in order[first : first + 4]]
            left = jnp.concatenate([gate_out[pick] for pick in picks], axis=0)
            right = jnp.concatenate([up_out[pick] for pick in picks], axis=0)
            target[...] = (
                jnp.dot(left, gate[:, columns], preferred_element_type=jnp.float32)
                + jnp.dot(right, up[:, columns], preferred_element_type=jnp.float32)
            ).astype(target.dtype)


def middle(part, other, one_hot, gate_weight, up_weight):
    local_ff, width = gate_weight.shape
    half, third = width // 2, width // 6
    rows = 8 * GROUP
    vmem_spec, any_spec = (pl.BlockSpec(memory_space=s) for s in (pltpu.VMEM, pl.ANY))
    small = jax.ShapeDtypeStruct((rows, local_ff), jnp.bfloat16)
    return pl.pallas_call(
        functools.partial(middle_kernel, third),
        out_shape=[jax.ShapeDtypeStruct((rows // 2, third), jnp.bfloat16)] * 3
        + [jax.ShapeDtypeStruct((rows // 2, third), jnp.float32)] * 3
        + [small] * 3,
        in_specs=[vmem_spec] * 3 + [any_spec] * 2,
        out_specs=[vmem_spec] * 9,
        scratch_shapes=[
            pltpu.VMEM((local_ff, half), jnp.bfloat16),
            pltpu.VMEM((local_ff, half), jnp.bfloat16),
            pltpu.SemaphoreType.DMA((6,)),
        ],
        compiler_params=pltpu.CompilerParams(vmem_limit_bytes=VMEM_LIMIT),
        cost_estimate=pl.CostEstimate(
            flops=4 * rows * local_ff * half, bytes_accessed=14 * 2**20, transcendentals=0
        ),
    )(part, other, one_hot, gate_weight, up_weight)


def weight_kernel(third, *refs):
    pieces, (gate_part, up_part, hidden) = refs[:24], refs[24:27]
    outs, (rows_in, rows_cot, results, sems, out_sems) = refs[27:30], refs[30:]
    copies = []
    for k in range(3):
        for label in range(8):
            piece = pieces[8 * k + label]
            for i, target in enumerate((rows_in, rows_cot)):
                copy = pltpu.make_async_copy(
                    piece.at[i],
                    target.at[pl.ds(GROUP * label, GROUP), pl.ds(k * third, third)],
                    sems.at[16 * k + 2 * label + i],
                )
                copy.start()
                copies.append(copy)
    out_copies = []
    for k in range(3):
        columns = slice(k * third, (k + 1) * third)
        for copy in copies[16 * k : 16 * k + 16]:
            copy.wait()
        for i, (left, rows) in enumerate(
            ((gate_part, rows_in), (up_part, rows_in), (hidden, rows_cot))
        ):
            results[i, :, columns] = lax.dot_general(
                left[...],
                rows[:, columns],
                (((0,), (0,)), ((), ())),
                preferred_element_type=jnp.float32,
            ).astype(jnp.bfloat16)
            copy = pltpu.make_async_copy(
                results.at[i, :, pl.ds(k * third, third)],
                outs[i].at[:, pl.ds(k * third, third)],
                out_sems.at[3 * k + i],
            )
            copy.start()
            out_copies.append(copy)
    for copy in out_copies:
        copy.wait()


def weight_grads(pieces, gate_part, up_part, hidden, third):
    rows, local_ff = gate_part.shape
    half = 3 * third
    vmem_spec, any_spec = (pl.BlockSpec(memory_space=s) for s in (pltpu.VMEM, pl.ANY))
    return pl.pallas_call(
        functools.partial(weight_kernel, third),
        out_shape=[jax.ShapeDtypeStruct((local_ff, half), jnp.bfloat16)] * 3,
        in_specs=[any_spec] * 24 + [vmem_spec] * 3,
        out_specs=[any_spec] * 3,
        scratch_shapes=[
            pltpu.VMEM((rows, half), jnp.bfloat16),
            pltpu.VMEM((rows, half), jnp.bfloat16),
            pltpu.VMEM((3, local_ff, half), jnp.bfloat16),
            pltpu.SemaphoreType.DMA((48,)),
            pltpu.SemaphoreType.DMA((9,)),
        ],
        compiler_params=pltpu.CompilerParams(vmem_limit_bytes=VMEM_LIMIT),
        cost_estimate=pl.CostEstimate(
            flops=6 * rows * local_ff * half, bytes_accessed=16 * 2**20, transcendentals=0
        ),
    )(*pieces, gate_part, up_part, hidden)


def cross_core_rows():
    matrix = np.zeros((8 * GROUP, 8 * GROUP), np.float32)
    for high in range(8):
        for low in range(8):
            for row in range(4):
                matrix[(high * 8 + low) * 4 + row, (low * 8 + high) * 4 + row] = 1.0
    return jnp.asarray(matrix, jnp.bfloat16)


def shards(inputs, cotangent, gate_weight, up_weight, down_weight):
    core = lax.axis_index("rep")
    width = inputs.shape[2]
    half, third = width // 2, width // 6
    micro = inputs.shape[0]

    rows = jnp.stack([inputs[:, 0], cotangent[:, 0]])
    low, high = rows[:, :, :half], rows[:, :, half:]
    mine = jnp.where(core == 0, low, high)
    theirs = send(jnp.where(core == 0, high, low), OTHER_CORE)
    block = jnp.concatenate(
        [jnp.where(core == 0, mine, theirs), jnp.where(core == 0, theirs, mine)], axis=1
    )
    block = jnp.concatenate(
        [block] + [send(block, neighbour(axes, 0)) for axes in ("x", "y", "xy")], axis=1
    )
    block = jnp.concatenate([block, send(block, neighbour("z", 0))], axis=1)
    pieces = []
    for k in range(3):
        held = [block[:, :, k * third : (k + 1) * third]]
        for axis in CHUNKS[k]:
            held = held + [send(piece, neighbour(axis, 1)) for piece in held]
        labelled = dict(zip(label_order(CHUNKS[k]), held))
        pieces += [labelled[label] for label in range(8)]

    part = forward(pieces, (gate_weight, up_weight, down_weight))
    other = send(part, OTHER_CORE)
    results = middle(part, other, cross_core_rows(), gate_weight, up_weight)
    outgoing, sums, (gate_part, up_part, hidden) = results[:3], results[3:6], results[6:]
    gate_grad, up_grad, down_grad = weight_grads(pieces, gate_part, up_part, hidden, third)

    for stage in (2, 1, 0):
        sums = [
            value + send(out, neighbour(CHUNKS[k][stage], 1)).astype(jnp.float32)
            for k, (value, out) in enumerate(zip(sums, outgoing))
        ]
        if stage:
            cut = sums[0].shape[0] // 2
            outgoing = [value[cut:].astype(jnp.bfloat16) for value in sums]
            sums = [value[:cut] for value in sums]
    value = jnp.concatenate(sums, axis=1)
    cut = value.shape[0] // 2
    value = value[:cut] + send(value[cut:].astype(jnp.bfloat16), neighbour("z", 0)).astype(
        jnp.float32
    )
    cut = value.shape[0] // 4
    value = value[:cut] + sum(
        send(value[i * cut : (i + 1) * cut].astype(jnp.bfloat16), neighbour(axes, 0)).astype(
            jnp.float32
        )
        for i, axes in ((1, "x"), (2, "y"), (3, "xy"))
    )
    value = value.astype(jnp.bfloat16)
    mine = jnp.where(core == 0, value[:micro], value[micro:])
    theirs = send(jnp.where(core == 0, value[micro:], value[:micro]), OTHER_CORE)
    input_grad = jnp.concatenate(
        [jnp.where(core == 0, mine, theirs), jnp.where(core == 0, theirs, mine)], axis=1
    )[:, None, :]
    return input_grad, gate_grad, up_grad, down_grad


def solution(mesh):
    return jax.shard_map(
        shards,
        mesh=mesh,
        in_specs=(
            P(None, ("rep", "tp", "att"), None),
            P(None, ("rep", "tp", "att"), None),
            P(("tp", "att"), None),
            P(("tp", "att"), None),
            P(("tp", "att"), None),
        ),
        out_specs=(
            P(None, ("rep", "tp", "att"), None),
            P(("tp", "att"), "rep"),
            P(("tp", "att"), "rep"),
            P(("tp", "att"), "rep"),
        ),
        check_vma=False,
    )
```

```python
import functools

import jax
import jax.numpy as jnp
import numpy as np
from jax import lax
from jax.experimental import pallas as pl
from jax.experimental.pallas import tpu as pltpu
from jax.sharding import PartitionSpec as P

AXES = ("rep", "tp", "att")
CHUNKS = (("x", "y", "z"), ("y", "z", "x"), ("z", "x", "y"))
CUBE = ("x", "y", "xy", "z", "xz", "yz", "xyz")
GROUP = 32
LANES = 256


def linear(core, x, y, z):
    return core * 64 + ((y % 2) * 16 + z * 4 + x) * 2 + y // 2


def pairs(moves, flip=0):
    result = []
    for core in range(2):
        dx, dy, dz = moves[core]
        for x in range(4):
            for y in range(4):
                for z in range(4):
                    result.append(
                        (linear(core, x, y, z), linear(core ^ flip, x ^ dx, y ^ dy, z ^ dz))
                    )
    return sorted(result)


def neighbour(axes, stage):
    moves = []
    for core in range(2):
        moves.append(
            tuple(
                (1 if core == stage else 3) if name in axes else 0
                for name in "xyz"
            )
        )
    return pairs(moves)


OTHER_CORE = pairs([(0, 0, 0)] * 2, flip=1)


def send(value, route):
    return lax.ppermute(value, AXES, route)


def label_order(axes):
    bit = {"x": 1, "y": 2, "z": 4}
    return [
        sum(bit[axis] for place, axis in enumerate(axes) if index >> place & 1)
        for index in range(8)
    ]


def call(kernel, operands, outs, scratch=(), limit=16, flops=0, megabytes=0):
    places = [place for place, _ in operands]
    values = [
        pltpu.with_memory_space_constraint(value, pltpu.VMEM if place == "vmem" else pltpu.HBM)
        for place, value in operands
    ]
    spec = {
        "vmem": pl.BlockSpec(memory_space=pltpu.VMEM),
        "hbm": pl.BlockSpec(memory_space=pltpu.HBM),
    }
    return pl.pallas_call(
        kernel,
        out_shape=[
            pltpu.VMEM(shape, dtype) if place == "vmem" else jax.ShapeDtypeStruct(shape, dtype)
            for place, shape, dtype in outs
        ],
        in_specs=[spec[place] for place in places],
        out_specs=[spec[place] for place, _, _ in outs],
        scratch_shapes=list(scratch),
        compiler_params=pltpu.CompilerParams(vmem_limit_bytes=limit * 2**20),
        cost_estimate=pl.CostEstimate(
            flops=flops, bytes_accessed=megabytes * 2**20, transcendentals=0
        ),
    )(*values)


def join_kernel(first, second, out):
    rows = first.shape[1]
    out[:, :rows] = first[...]
    out[:, rows:] = second[...]


def join(first, second):
    shape = (first.shape[0], 2 * first.shape[1], first.shape[2])
    return call(
        join_kernel,
        [("vmem", first), ("vmem", second)],
        [("vmem", shape, first.dtype)],
        megabytes=2,
    )[0]


def add_products(third, k, first, piece, weights, acc):
    columns = slice(k * third, (k + 1) * third)
    order = label_order(CHUNKS[k])[first : first + 4]
    for i, source in enumerate((0, 0, 1)):
        product = lax.dot_general(
            piece[source],
            weights[i][:, columns],
            (((1,), (1,)), ((), ())),
            preferred_element_type=jnp.float32,
        )
        local_ff = product.shape[1]
        for place, label in enumerate(order):
            rows = slice(GROUP * label, GROUP * label + GROUP)
            acc[rows, i * LANES : i * LANES + local_ff] += product[
                GROUP * place : GROUP * place + GROUP
            ]


def load_kernel(third, *refs):
    hbm, weights, sems = refs[:3], refs[3:6], refs[6]
    start = lax.axis_index("rep") * (3 * third)
    copies = []
    for i in range(3):
        copy = pltpu.make_async_copy(
            hbm[i].at[:, pl.ds(pl.multiple_of(start, third), 3 * third)], weights[i], sems.at[i]
        )
        copy.start()
        copies.append(copy)
    for copy in copies:
        copy.wait()


def early_kernel(third, *refs):
    pieces, weights, acc = refs[:3], refs[3:6], refs[6]
    acc[...] = jnp.zeros_like(acc)
    for k in range(3):
        add_products(third, k, 0, pieces[k], weights, acc)


def late_kernel(third, k, *refs):
    piece, weights, acc, out = refs[0], refs[1:4], refs[4], refs[5]
    out[...] = acc[...]
    add_products(third, k, 4, piece, weights, out)


def permuted(one_hot, value):
    high = value.astype(jnp.bfloat16)
    rest = value - high.astype(jnp.float32)
    middle = rest.astype(jnp.bfloat16)
    low = (rest - middle.astype(jnp.float32)).astype(jnp.bfloat16)
    return (
        jnp.dot(one_hot, high, preferred_element_type=jnp.float32)
        + jnp.dot(one_hot, middle, preferred_element_type=jnp.float32)
        + jnp.dot(one_hot, low, preferred_element_type=jnp.float32)
    )


def input_products(third, first, gate_part, up_part, gate, up, targets):
    for k in range(3):
        columns = slice(k * third, (k + 1) * third)
        picks = [
            slice(GROUP * label, GROUP * label + GROUP)
            for label in label_order(CHUNKS[k])[first : first + 4]
        ]
        left = jnp.concatenate([gate_part[pick] for pick in picks], axis=0)
        right = jnp.concatenate([up_part[pick] for pick in picks], axis=0)
        targets[k][...] = (
            jnp.dot(left, gate[:, columns], preferred_element_type=jnp.float32)
            + jnp.dot(right, up[:, columns], preferred_element_type=jnp.float32)
        ).astype(targets[k].dtype)


def middle_kernel(third, *refs):
    part, other, one_hot, gate, up = refs[:5]
    sends, (gate_out, up_out, hidden_out) = refs[5:8], refs[8:11]
    local_ff = gate.shape[0]
    matrix = one_hot[...]
    total = [
        part[:, i * LANES : (i + 1) * LANES]
        + permuted(matrix, other[:, i * LANES : (i + 1) * LANES])
        for i in range(3)
    ]
    pre_gate, pre_up, hidden_grad = (value[:, :local_ff] for value in total)
    sig = jax.nn.sigmoid(pre_gate)
    act = pre_gate * sig
    hidden_out[...] = (act * pre_up).astype(jnp.bfloat16)
    gate_out[...] = (hidden_grad * pre_up * sig * (1.0 + pre_gate * (1.0 - sig))).astype(
        jnp.bfloat16
    )
    up_out[...] = (hidden_grad * act).astype(jnp.bfloat16)
    input_products(third, 4, gate_out, up_out, gate, up, sends)


def rest_kernel(third, *refs):
    pieces, (gate, up, gate_part, up_part, hidden) = refs[:6], refs[6:11]
    keeps, outs, (results, sems) = refs[11:14], refs[14:17], refs[17:]
    input_products(third, 0, gate_part, up_part, gate, up, keeps)
    copies = []
    for k in range(3):
        order = label_order(CHUNKS[k])
        for i, (left, source) in enumerate(((gate_part, 0), (up_part, 0), (hidden, 1))):
            groups = [
                piece[source, i * GROUP : (i + 1) * GROUP]
                for piece in pieces[2 * k : 2 * k + 2]
                for i in range(4)
            ]
            rows = jnp.concatenate([groups[order.index(label)] for label in range(8)], axis=0)
            results[i, :, k * third : (k + 1) * third] = lax.dot_general(
                left[...], rows, (((0,), (0,)), ((), ())), preferred_element_type=jnp.float32
            ).astype(jnp.bfloat16)
            copy = pltpu.make_async_copy(
                results.at[i, :, pl.ds(k * third, third)],
                outs[i].at[:, pl.ds(k * third, third)],
                sems.at[3 * k + i],
            )
            copy.start()
            copies.append(copy)
    for copy in copies:
        copy.wait()


def cross_core_rows():
    matrix = np.zeros((8 * GROUP, 8 * GROUP), np.float32)
    for high in range(8):
        for low in range(8):
            for row in range(4):
                matrix[(high * 8 + low) * 4 + row, (low * 8 + high) * 4 + row] = 1.0
    return jnp.asarray(matrix, jnp.bfloat16)


def shards(inputs, cotangent, gate_weight, up_weight, down_weight):
    core = lax.axis_index("rep")
    width = inputs.shape[2]
    half, third = width // 2, width // 6
    micro = inputs.shape[0]

    rows = jnp.stack([inputs[:, 0], cotangent[:, 0]])
    low, high = rows[:, :, :half], rows[:, :, half:]
    mine = jnp.where(core == 0, low, high)
    theirs = send(jnp.where(core == 0, high, low), OTHER_CORE)
    block = jnp.concatenate(
        [jnp.where(core == 0, mine, theirs), jnp.where(core == 0, theirs, mine)], axis=1
    )
    block = jnp.concatenate(
        [block] + [send(block, neighbour(axes, 0)) for axes in CUBE], axis=1
    )
    local_ff = gate_weight.shape[0]
    rows = 8 * GROUP
    vmem, hbm = (lambda value: ("vmem", value)), (lambda value: ("hbm", value))
    fourth = [
        send(block[:, :, k * third : (k + 1) * third], neighbour(CHUNKS[k][0], 1))
        for k in range(3)
    ]
    weights = call(
        functools.partial(load_kernel, third),
        [hbm(gate_weight), hbm(up_weight), hbm(down_weight)],
        [("vmem", (local_ff, half), jnp.bfloat16)] * 3,
        [pltpu.SemaphoreType.DMA((3,))],
        megabytes=16,
    )
    fourth, weights = lax.optimization_barrier((fourth, weights))
    held, last = [], []
    for k in range(3):
        own = block[:, :, k * third : (k + 1) * third]
        for stage, axis in enumerate(CHUNKS[k]):
            new = fourth[k] if stage == 0 else send(own, neighbour(axis, 1))
            if stage < 2:
                own = join(own, new)
        held.append(own)
        last.append(new)
    (part,) = call(
        functools.partial(early_kernel, third),
        [vmem(value) for value in (*held, *weights)],
        [("vmem", (rows, 3 * LANES), jnp.float32)],
        flops=3 * rows * local_ff * half,
        megabytes=14,
    )
    for k in range(3):
        (part,) = call(
            functools.partial(late_kernel, third, k),
            [vmem(value) for value in (last[k], *weights, part)],
            [("vmem", (rows, 3 * LANES), jnp.float32)],
            flops=rows * local_ff * half,
            megabytes=5,
        )
    other = send(part, OTHER_CORE)
    small = ("vmem", (rows, local_ff), jnp.bfloat16)
    results = call(
        functools.partial(middle_kernel, third),
        [vmem(value) for value in (part, other, cross_core_rows(), weights[0], weights[1])],
        [("vmem", (rows // 2, third), jnp.bfloat16)] * 3 + [small] * 3,
        flops=2 * rows * local_ff * half,
        megabytes=8,
    )
    outgoing, parts = results[:3], results[3:]
    received = [send(out, neighbour(CHUNKS[k][2], 1)) for k, out in enumerate(outgoing)]
    results = call(
        functools.partial(rest_kernel, third),
        [vmem(piece) for k in range(3) for piece in (held[k], last[k])]
        + [vmem(value) for value in (weights[0], weights[1], *parts)],
        [("vmem", (rows // 2, third), jnp.float32)] * 3
        + [("hbm", (local_ff, half), jnp.bfloat16)] * 3,
        [pltpu.VMEM((3, local_ff, half), jnp.bfloat16), pltpu.SemaphoreType.DMA((9,))],
        limit=24,
        flops=8 * rows * local_ff * half,
        megabytes=24,
    )
    sums, (gate_grad, up_grad, down_grad) = results[:3], results[3:]

    for stage in (2, 1, 0):
        sums = [value + new.astype(jnp.float32) for value, new in zip(sums, received)]
        if stage:
            cut = sums[0].shape[0] // 2
            received = [
                send(value[cut:].astype(jnp.bfloat16), neighbour(CHUNKS[k][stage - 1], 1))
                for k, value in enumerate(sums)
            ]
            sums = [value[:cut] for value in sums]
    value = jnp.concatenate(sums, axis=1)
    cut = value.shape[0] // 8
    value = value[:cut] + sum(
        send(value[i * cut : (i + 1) * cut].astype(jnp.bfloat16), neighbour(axes, 0)).astype(
            jnp.float32
        )
        for i, axes in enumerate(CUBE, 1)
    )
    value = value.astype(jnp.bfloat16)
    mine = jnp.where(core == 0, value[:micro], value[micro:])
    theirs = send(jnp.where(core == 0, value[micro:], value[:micro]), OTHER_CORE)
    input_grad = jnp.concatenate(
        [jnp.where(core == 0, mine, theirs), jnp.where(core == 0, theirs, mine)], axis=1
    )[:, None, :]
    return input_grad, gate_grad, up_grad, down_grad


def solution(mesh):
    return jax.shard_map(
        shards,
        mesh=mesh,
        in_specs=(
            P(None, ("rep", "tp", "att"), None),
            P(None, ("rep", "tp", "att"), None),
            P(("tp", "att"), None),
            P(("tp", "att"), None),
            P(("tp", "att"), None),
        ),
        out_specs=(
            P(None, ("rep", "tp", "att"), None),
            P(("tp", "att"), "rep"),
            P(("tp", "att"), "rep"),
            P(("tp", "att"), "rep"),
        ),
        check_vma=False,
    )
```

```python
import functools

import jax
import jax.numpy as jnp
import numpy as np
from jax import lax
from jax.experimental import pallas as pl
from jax.experimental.pallas import tpu as pltpu
from jax.sharding import PartitionSpec as P

AXES = ("rep", "tp", "att")
CHUNKS = (("x", "y", "z"), ("y", "z", "x"), ("z", "x", "y"))
SCATTER_NEARER = "xy"
CUBE = ("x", "y", "xy", "z", "xz", "yz", "xyz")
GROUP = 32
LANES = 256


def linear(core, x, y, z):
    return core * 64 + ((y % 2) * 16 + z * 4 + x) * 2 + y // 2


def pairs(moves, flip=0):
    result = []
    for core in range(2):
        dx, dy, dz = moves[core]
        for x in range(4):
            for y in range(4):
                for z in range(4):
                    result.append(
                        (linear(core, x, y, z), linear(core ^ flip, x ^ dx, y ^ dy, z ^ dz))
                    )
    return sorted(result)


def neighbour(axes, stage, nearer="xyz"):
    moves = []
    for core in range(2):
        moves.append(
            tuple(
                (1 if core == stage ^ (name not in nearer) else 3) if name in axes else 0
                for name in "xyz"
            )
        )
    return pairs(moves)


OTHER_CORE = pairs([(0, 0, 0)] * 2, flip=1)


def send(value, route):
    return lax.ppermute(value, AXES, route)


def label_order(axes):
    bit = {"x": 1, "y": 2, "z": 4}
    return [
        sum(bit[axis] for place, axis in enumerate(axes) if index >> place & 1)
        for index in range(8)
    ]


def call(kernel, operands, outs, scratch=(), limit=16, flops=0, megabytes=0):
    places = [place for place, _ in operands]
    values = [
        pltpu.with_memory_space_constraint(value, pltpu.VMEM if place == "vmem" else pltpu.HBM)
        for place, value in operands
    ]
    spec = {
        "vmem": pl.BlockSpec(memory_space=pltpu.VMEM),
        "hbm": pl.BlockSpec(memory_space=pltpu.HBM),
    }
    return pl.pallas_call(
        kernel,
        out_shape=[
            pltpu.VMEM(shape, dtype) if place == "vmem" else jax.ShapeDtypeStruct(shape, dtype)
            for place, shape, dtype in outs
        ],
        in_specs=[spec[place] for place in places],
        out_specs=[spec[place] for place, _, _ in outs],
        scratch_shapes=list(scratch),
        compiler_params=pltpu.CompilerParams(vmem_limit_bytes=limit * 2**20),
        cost_estimate=pl.CostEstimate(
            flops=flops, bytes_accessed=megabytes * 2**20, transcendentals=0
        ),
    )(*values)


def join_kernel(first, second, out):
    rows = first.shape[1]
    out[:, :rows] = first[...]
    out[:, rows:] = second[...]


def join(first, second):
    shape = (first.shape[0], 2 * first.shape[1], first.shape[2])
    return call(
        join_kernel,
        [("vmem", first), ("vmem", second)],
        [("vmem", shape, first.dtype)],
        megabytes=2,
    )[0]


def add_products(third, k, first, piece, weights, acc):
    columns = slice(k * third, (k + 1) * third)
    order = label_order(CHUNKS[k])[first : first + 4]
    for i, source in enumerate((0, 0, 1)):
        product = lax.dot_general(
            piece[source],
            weights[i][:, columns],
            (((1,), (1,)), ((), ())),
            preferred_element_type=jnp.float32,
        )
        local_ff = product.shape[1]
        for place, label in enumerate(order):
            rows = slice(GROUP * label, GROUP * label + GROUP)
            acc[rows, i * LANES : i * LANES + local_ff] += product[
                GROUP * place : GROUP * place + GROUP
            ]


def load_kernel(third, *refs):
    hbm, weights, sems = refs[:3], refs[3:6], refs[6]
    start = lax.axis_index("rep") * (3 * third)
    copies = []
    for i in range(3):
        copy = pltpu.make_async_copy(
            hbm[i].at[:, pl.ds(pl.multiple_of(start, third), 3 * third)], weights[i], sems.at[i]
        )
        copy.start()
        copies.append(copy)
    for copy in copies:
        copy.wait()


def early_kernel(third, *refs):
    pieces, weights, acc = refs[:3], refs[3:6], refs[6]
    acc[...] = jnp.zeros_like(acc)
    for k in range(3):
        add_products(third, k, 0, pieces[k], weights, acc)


def late_kernel(third, k, *refs):
    piece, weights, acc, out = refs[0], refs[1:4], refs[4], refs[5]
    out[...] = acc[...]
    add_products(third, k, 4, piece, weights, out)


def permuted(one_hot, value):
    high = value.astype(jnp.bfloat16)
    rest = value - high.astype(jnp.float32)
    middle = rest.astype(jnp.bfloat16)
    low = (rest - middle.astype(jnp.float32)).astype(jnp.bfloat16)
    return (
        jnp.dot(one_hot, high, preferred_element_type=jnp.float32)
        + jnp.dot(one_hot, middle, preferred_element_type=jnp.float32)
        + jnp.dot(one_hot, low, preferred_element_type=jnp.float32)
    )


def input_products(third, first, gate_part, up_part, gate, up, targets):
    for k in range(3):
        columns = slice(k * third, (k + 1) * third)
        picks = [
            slice(GROUP * label, GROUP * label + GROUP)
            for label in label_order(CHUNKS[k])[first : first + 4]
        ]
        left = jnp.concatenate([gate_part[pick] for pick in picks], axis=0)
        right = jnp.concatenate([up_part[pick] for pick in picks], axis=0)
        targets[k][...] = (
            jnp.dot(left, gate[:, columns], preferred_element_type=jnp.float32)
            + jnp.dot(right, up[:, columns], preferred_element_type=jnp.float32)
        ).astype(targets[k].dtype)


def middle_kernel(third, *refs):
    part, other, cross_core, scatter, gate, up = refs[:6]
    sends, (gate_out, up_out, hidden_out, gate_sums, up_sums) = refs[6:9], refs[9:14]
    local_ff = gate.shape[0]
    matrix = cross_core[...]
    total = [
        part[:, i * LANES : (i + 1) * LANES]
        + permuted(matrix, other[:, i * LANES : (i + 1) * LANES])
        for i in range(3)
    ]
    pre_gate, pre_up, hidden_grad = (value[:, :local_ff] for value in total)
    sig = jax.nn.sigmoid(pre_gate)
    act = pre_gate * sig
    hidden_out[...] = (act * pre_up).astype(jnp.bfloat16)
    gate_out[...] = (hidden_grad * pre_up * sig * (1.0 + pre_gate * (1.0 - sig))).astype(
        jnp.bfloat16
    )
    up_out[...] = (hidden_grad * act).astype(jnp.bfloat16)
    for source, target in ((gate_out, gate_sums), (up_out, up_sums)):
        target[...] = jnp.dot(
            scatter[...], source[...], preferred_element_type=jnp.float32
        ).astype(jnp.bfloat16)
    input_products(third, 4, gate_sums, up_sums, gate, up, sends)


def keep_kernel(third, gate_sums, up_sums, gate, up, *keeps):
    input_products(third, 0, gate_sums, up_sums, gate, up, keeps)


def weight_kernel(third, *refs):
    pieces, (gate_part, up_part, hidden) = refs[:6], refs[6:9]
    outs, (results, sems) = refs[9:12], refs[12:]
    copies = []
    for k in range(3):
        order = label_order(CHUNKS[k])
        for i, (left, source) in enumerate(((gate_part, 0), (up_part, 0), (hidden, 1))):
            groups = [
                piece[source, i * GROUP : (i + 1) * GROUP]
                for piece in pieces[2 * k : 2 * k + 2]
                for i in range(4)
            ]
            rows = jnp.concatenate([groups[order.index(label)] for label in range(8)], axis=0)
            results[i, :, k * third : (k + 1) * third] = lax.dot_general(
                left[...], rows, (((0,), (0,)), ((), ())), preferred_element_type=jnp.float32
            ).astype(jnp.bfloat16)
            copy = pltpu.make_async_copy(
                results.at[i, :, pl.ds(k * third, third)],
                outs[i].at[:, pl.ds(k * third, third)],
                sems.at[3 * k + i],
            )
            copy.start()
            copies.append(copy)
    for copy in copies:
        copy.wait()


def exchanged_rows(axes):
    mask = sum({"x": 1, "y": 2, "z": 4}[axis] for axis in axes)
    matrix = np.zeros((8 * GROUP, 8 * GROUP), np.float32)
    for high in range(8):
        for low in range(8):
            new_high, new_low = high & ~mask | low & mask, low & ~mask | high & mask
            for row in range(4):
                matrix[(high * 8 + low) * 4 + row, (new_high * 8 + new_low) * 4 + row] = 1.0
    return jnp.asarray(matrix, jnp.bfloat16)


def shards(inputs, cotangent, gate_weight, up_weight, down_weight):
    core = lax.axis_index("rep")
    width = inputs.shape[2]
    half, third = width // 2, width // 6
    micro = inputs.shape[0]

    rows = jnp.stack([inputs[:, 0], cotangent[:, 0]])
    low, high = rows[:, :, :half], rows[:, :, half:]
    mine = jnp.where(core == 0, low, high)
    theirs = send(jnp.where(core == 0, high, low), OTHER_CORE)
    block = jnp.concatenate(
        [jnp.where(core == 0, mine, theirs), jnp.where(core == 0, theirs, mine)], axis=1
    )
    block = jnp.concatenate(
        [block] + [send(block, neighbour(axes, 0)) for axes in CUBE], axis=1
    )
    local_ff = gate_weight.shape[0]
    rows = 8 * GROUP
    vmem, hbm = (lambda value: ("vmem", value)), (lambda value: ("hbm", value))
    weights = call(
        functools.partial(load_kernel, third),
        [hbm(gate_weight), hbm(up_weight), hbm(down_weight)],
        [("vmem", (local_ff, half), jnp.bfloat16)] * 3,
        [pltpu.SemaphoreType.DMA((3,))],
        megabytes=16,
    )
    held = [block[:, :, k * third : (k + 1) * third] for k in range(3)]
    for stage in range(3):
        last = [send(held[k], neighbour(CHUNKS[k][stage], 1)) for k in range(3)]
        if stage == 1:
            last[0], weights = lax.optimization_barrier((last[0], weights))
        if stage < 2:
            held = [join(own, new) for own, new in zip(held, last)]
    (part,) = call(
        functools.partial(early_kernel, third),
        [vmem(value) for value in (*held, *weights)],
        [("vmem", (rows, 3 * LANES), jnp.float32)],
        flops=3 * rows * local_ff * half,
        megabytes=14,
    )
    for k in range(3):
        (part,) = call(
            functools.partial(late_kernel, third, k),
            [vmem(value) for value in (last[k], *weights, part)],
            [("vmem", (rows, 3 * LANES), jnp.float32)],
            flops=rows * local_ff * half,
            megabytes=5,
        )
    other = send(part, OTHER_CORE)
    small = ("vmem", (rows, local_ff), jnp.bfloat16)
    scattered = "".join(axis for axis in "xyz" if axis not in SCATTER_NEARER)
    operands = (
        part,
        other,
        exchanged_rows("xyz"),
        exchanged_rows(scattered),
        weights[0],
        weights[1],
    )
    results = call(
        functools.partial(middle_kernel, third),
        [vmem(value) for value in operands],
        [("vmem", (rows // 2, third), jnp.bfloat16)] * 3 + [small] * 5,
        flops=2 * rows * local_ff * half,
        megabytes=8,
    )
    outgoing, parts = results[:3], results[3:]
    received = [send(out, neighbour(CHUNKS[k][2], 1, SCATTER_NEARER)) for k, out in enumerate(outgoing)]
    sums = call(
        functools.partial(keep_kernel, third),
        [vmem(value) for value in (*parts[3:], weights[0], weights[1])],
        [("vmem", (rows // 2, third), jnp.float32)] * 3,
        flops=2 * rows * local_ff * half,
        megabytes=8,
    )

    for stage in (2, 1, 0):
        sums = [value + new.astype(jnp.float32) for value, new in zip(sums, received)]
        if stage:
            cut = sums[0].shape[0] // 2
            received = [
                send(value[cut:].astype(jnp.bfloat16), neighbour(CHUNKS[k][stage - 1], 1, SCATTER_NEARER))
                for k, value in enumerate(sums)
            ]
            sums = [value[:cut] for value in sums]
    value = jnp.concatenate(sums, axis=1)
    cut = value.shape[0] // 2
    leaving, parts = lax.optimization_barrier((value[cut:].astype(jnp.bfloat16), parts))
    arriving = send(leaving, neighbour("z", 0, SCATTER_NEARER))
    grads = call(
        functools.partial(weight_kernel, third),
        [vmem(piece) for k in range(3) for piece in (held[k], last[k])]
        + [vmem(value) for value in parts[:3]],
        [("hbm", (local_ff, half), jnp.bfloat16)] * 3,
        [pltpu.VMEM((3, local_ff, half), jnp.bfloat16), pltpu.SemaphoreType.DMA((9,))],
        limit=24,
        flops=6 * rows * local_ff * half,
        megabytes=24,
    )
    arriving, (gate_grad, up_grad, down_grad) = lax.optimization_barrier((arriving, grads))
    value = value[:cut] + arriving.astype(jnp.float32)
    cut = value.shape[0] // 4
    value = value[:cut] + sum(
        send(value[i * cut : (i + 1) * cut].astype(jnp.bfloat16), neighbour(axes, 0, SCATTER_NEARER)).astype(
            jnp.float32
        )
        for i, axes in ((1, "x"), (2, "y"), (3, "xy"))
    )
    value = value.astype(jnp.bfloat16)
    mine = jnp.where(core == 0, value[:micro], value[micro:])
    theirs = send(jnp.where(core == 0, value[micro:], value[:micro]), OTHER_CORE)
    input_grad = jnp.concatenate(
        [jnp.where(core == 0, mine, theirs), jnp.where(core == 0, theirs, mine)], axis=1
    )[:, None, :]
    return input_grad, gate_grad, up_grad, down_grad


def solution(mesh):
    return jax.shard_map(
        shards,
        mesh=mesh,
        in_specs=(
            P(None, ("rep", "tp", "att"), None),
            P(None, ("rep", "tp", "att"), None),
            P(("tp", "att"), None),
            P(("tp", "att"), None),
            P(("tp", "att"), None),
        ),
        out_specs=(
            P(None, ("rep", "tp", "att"), None),
            P(("tp", "att"), "rep"),
            P(("tp", "att"), "rep"),
            P(("tp", "att"), "rep"),
        ),
        check_vma=False,
    )
```

```python
import functools

import jax
import jax.numpy as jnp
import numpy as np
from jax import lax
from jax.experimental import pallas as pl
from jax.experimental.pallas import tpu as pltpu
from jax.sharding import PartitionSpec as P

AXES = ("rep", "tp", "att")
CHUNKS = (("x", "y", "z"), ("y", "z", "x"), ("z", "x", "y"))
SCATTER_NEARER = "xy"
CUBE = ("x", "y", "xy", "z", "xz", "yz", "xyz")
GROUP = 32
LANES = 256


def linear(core, x, y, z):
    return core * 64 + ((y % 2) * 16 + z * 4 + x) * 2 + y // 2


def pairs(moves, flip=0):
    result = []
    for core in range(2):
        dx, dy, dz = moves[core]
        for x in range(4):
            for y in range(4):
                for z in range(4):
                    result.append(
                        (linear(core, x, y, z), linear(core ^ flip, x ^ dx, y ^ dy, z ^ dz))
                    )
    return sorted(result)


def neighbour(axes, stage, nearer="xyz"):
    moves = []
    for core in range(2):
        moves.append(
            tuple(
                (1 if core == stage ^ (name not in nearer) else 3) if name in axes else 0
                for name in "xyz"
            )
        )
    return pairs(moves)


OTHER_CORE = pairs([(0, 0, 0)] * 2, flip=1)


def send(value, route):
    return lax.ppermute(value, AXES, route)


def label_order(axes):
    bit = {"x": 1, "y": 2, "z": 4}
    return [
        sum(bit[axis] for place, axis in enumerate(axes) if index >> place & 1)
        for index in range(8)
    ]


def call(kernel, operands, outs, scratch=(), limit=16, flops=0, megabytes=0, aliases=None):
    places = [place for place, _ in operands]
    values = [
        pltpu.with_memory_space_constraint(value, pltpu.VMEM if place == "vmem" else pltpu.HBM)
        for place, value in operands
    ]
    spec = {
        "vmem": pl.BlockSpec(memory_space=pltpu.VMEM),
        "hbm": pl.BlockSpec(memory_space=pltpu.HBM),
    }
    return pl.pallas_call(
        kernel,
        out_shape=[
            pltpu.VMEM(shape, dtype) if place == "vmem" else jax.ShapeDtypeStruct(shape, dtype)
            for place, shape, dtype in outs
        ],
        in_specs=[spec[place] for place in places],
        out_specs=[spec[place] for place, _, _ in outs],
        scratch_shapes=list(scratch),
        input_output_aliases=aliases or {},
        compiler_params=pltpu.CompilerParams(vmem_limit_bytes=limit * 2**20),
        cost_estimate=pl.CostEstimate(
            flops=flops, bytes_accessed=megabytes * 2**20, transcendentals=0
        ),
    )(*values)


def join_kernel(first, second, out):
    rows = first.shape[1]
    out[:, :rows] = first[...]
    out[:, rows:] = second[...]


def join(first, second):
    shape = (first.shape[0], 2 * first.shape[1], first.shape[2])
    return call(
        join_kernel,
        [("vmem", first), ("vmem", second)],
        [("vmem", shape, first.dtype)],
        megabytes=2,
    )[0]


def add_products(third, k, first, piece, weights, acc):
    columns = slice(k * third, (k + 1) * third)
    order = label_order(CHUNKS[k])[first : first + 4]
    for i, source in enumerate((0, 0, 1)):
        product = lax.dot_general(
            piece[source],
            weights[i][:, columns],
            (((1,), (1,)), ((), ())),
            preferred_element_type=jnp.float32,
        )
        local_ff = product.shape[1]
        for place, label in enumerate(order):
            rows = slice(GROUP * label, GROUP * label + GROUP)
            acc[rows, i * LANES : i * LANES + local_ff] += product[
                GROUP * place : GROUP * place + GROUP
            ]


def load_kernel(third, *refs):
    hbm, weights, sems = refs[:3], refs[3:6], refs[6]
    start = lax.axis_index("rep") * (3 * third)
    copies = []
    for i in range(3):
        copy = pltpu.make_async_copy(
            hbm[i].at[:, pl.ds(pl.multiple_of(start, third), 3 * third)], weights[i], sems.at[i]
        )
        copy.start()
        copies.append(copy)
    for copy in copies:
        copy.wait()


def early_kernel(third, *refs):
    pieces, weights, acc = refs[:3], refs[3:6], refs[6]
    acc[...] = jnp.zeros_like(acc)
    for k in range(3):
        add_products(third, k, 0, pieces[k], weights, acc)


def late_kernel(third, k, *refs):
    piece, weights, out = refs[0], refs[1:4], refs[5]
    add_products(third, k, 4, piece, weights, out)


def permuted(one_hot, value):
    high = value.astype(jnp.bfloat16)
    rest = value - high.astype(jnp.float32)
    middle = rest.astype(jnp.bfloat16)
    low = (rest - middle.astype(jnp.float32)).astype(jnp.bfloat16)
    return (
        jnp.dot(one_hot, high, preferred_element_type=jnp.float32)
        + jnp.dot(one_hot, middle, preferred_element_type=jnp.float32)
        + jnp.dot(one_hot, low, preferred_element_type=jnp.float32)
    )


def input_products(third, first, gate_part, up_part, gate, up, targets):
    for k in range(3):
        columns = slice(k * third, (k + 1) * third)
        picks = [
            slice(GROUP * label, GROUP * label + GROUP)
            for label in label_order(CHUNKS[k])[first : first + 4]
        ]
        left = jnp.concatenate([gate_part[pick] for pick in picks], axis=0)
        right = jnp.concatenate([up_part[pick] for pick in picks], axis=0)
        targets[k][...] = (
            jnp.dot(left, gate[:, columns], preferred_element_type=jnp.float32)
            + jnp.dot(right, up[:, columns], preferred_element_type=jnp.float32)
        ).astype(targets[k].dtype)


def middle_kernel(third, *refs):
    part, other, cross_core, scatter, gate, up = refs[:6]
    sends, (gate_out, up_out, hidden_out, gate_sums, up_sums) = refs[6:9], refs[9:14]
    local_ff = gate.shape[0]
    matrix = cross_core[...]
    total = [
        part[:, i * LANES : (i + 1) * LANES]
        + permuted(matrix, other[:, i * LANES : (i + 1) * LANES])
        for i in range(3)
    ]
    pre_gate, pre_up, hidden_grad = (value[:, :local_ff] for value in total)
    sig = jax.nn.sigmoid(pre_gate)
    act = pre_gate * sig
    hidden_out[...] = (act * pre_up).astype(jnp.bfloat16)
    gate_out[...] = (hidden_grad * pre_up * sig * (1.0 + pre_gate * (1.0 - sig))).astype(
        jnp.bfloat16
    )
    up_out[...] = (hidden_grad * act).astype(jnp.bfloat16)
    for source, target in ((gate_out, gate_sums), (up_out, up_sums)):
        target[...] = jnp.dot(
            scatter[...], source[...], preferred_element_type=jnp.float32
        ).astype(jnp.bfloat16)
    input_products(third, 4, gate_sums, up_sums, gate, up, sends)


def keep_kernel(third, gate_sums, up_sums, gate, up, *keeps):
    input_products(third, 0, gate_sums, up_sums, gate, up, keeps)


def weight_kernel(third, *refs):
    pieces, (gate_part, up_part, hidden) = refs[:6], refs[6:9]
    outs, (results, sems) = refs[9:12], refs[12:]
    copies = []
    for k in range(3):
        order = label_order(CHUNKS[k])
        for i, (left, source) in enumerate(((gate_part, 0), (up_part, 0), (hidden, 1))):
            groups = [
                piece[source, i * GROUP : (i + 1) * GROUP]
                for piece in pieces[2 * k : 2 * k + 2]
                for i in range(4)
            ]
            rows = jnp.concatenate([groups[order.index(label)] for label in range(8)], axis=0)
            results[i, :, k * third : (k + 1) * third] = lax.dot_general(
                left[...], rows, (((0,), (0,)), ((), ())), preferred_element_type=jnp.float32
            ).astype(jnp.bfloat16)
            copy = pltpu.make_async_copy(
                results.at[i, :, pl.ds(k * third, third)],
                outs[i].at[:, pl.ds(k * third, third)],
                sems.at[3 * k + i],
            )
            copy.start()
            copies.append(copy)
    for copy in copies:
        copy.wait()


def exchanged_rows(axes):
    mask = sum({"x": 1, "y": 2, "z": 4}[axis] for axis in axes)
    matrix = np.zeros((8 * GROUP, 8 * GROUP), np.float32)
    for high in range(8):
        for low in range(8):
            new_high, new_low = high & ~mask | low & mask, low & ~mask | high & mask
            for row in range(4):
                matrix[(high * 8 + low) * 4 + row, (new_high * 8 + new_low) * 4 + row] = 1.0
    return jnp.asarray(matrix, jnp.bfloat16)


def shards(inputs, cotangent, gate_weight, up_weight, down_weight):
    core = lax.axis_index("rep")
    width = inputs.shape[2]
    half, third = width // 2, width // 6
    micro = inputs.shape[0]

    mine = jnp.stack([inputs[:, 0], cotangent[:, 0]])
    theirs = jnp.stack([send(inputs, OTHER_CORE)[:, 0], send(cotangent, OTHER_CORE)[:, 0]])
    first = jnp.concatenate([mine[:, :, :half], theirs[:, :, :half]], axis=1)
    second = jnp.concatenate([theirs[:, :, half:], mine[:, :, half:]], axis=1)
    block = jnp.where(core == 0, first, second)
    block = jnp.concatenate(
        [block] + [send(block, neighbour(axes, 0)) for axes in CUBE], axis=1
    )
    local_ff = gate_weight.shape[0]
    rows = 8 * GROUP
    vmem, hbm = (lambda value: ("vmem", value)), (lambda value: ("hbm", value))
    weights = call(
        functools.partial(load_kernel, third),
        [hbm(gate_weight), hbm(up_weight), hbm(down_weight)],
        [("vmem", (local_ff, half), jnp.bfloat16)] * 3,
        [pltpu.SemaphoreType.DMA((3,))],
        megabytes=16,
    )
    held = [block[:, :, k * third : (k + 1) * third] for k in range(3)]
    for stage in range(3):
        last = [send(held[k], neighbour(CHUNKS[k][stage], 1)) for k in range(3)]
        if stage == 1:
            last[0], weights = lax.optimization_barrier((last[0], weights))
        if stage < 2:
            held = [join(own, new) for own, new in zip(held, last)]
    (part,) = call(
        functools.partial(early_kernel, third),
        [vmem(value) for value in (*held, *weights)],
        [("vmem", (rows, 3 * LANES), jnp.float32)],
        flops=3 * rows * local_ff * half,
        megabytes=14,
    )
    for k in range(3):
        (part,) = call(
            functools.partial(late_kernel, third, k),
            [vmem(value) for value in (last[k], *weights, part)],
            [("vmem", (rows, 3 * LANES), jnp.float32)],
            flops=rows * local_ff * half,
            megabytes=5,
            aliases={4: 0},
        )
    other = send(part, OTHER_CORE)
    small = ("vmem", (rows, local_ff), jnp.bfloat16)
    scattered = "".join(axis for axis in "xyz" if axis not in SCATTER_NEARER)
    operands = (
        part,
        other,
        exchanged_rows("xyz"),
        exchanged_rows(scattered),
        weights[0],
        weights[1],
    )
    results = call(
        functools.partial(middle_kernel, third),
        [vmem(value) for value in operands],
        [("vmem", (rows // 2, third), jnp.bfloat16)] * 3 + [small] * 5,
        flops=2 * rows * local_ff * half,
        megabytes=8,
    )
    outgoing, parts = results[:3], results[3:]
    received = [send(out, neighbour(CHUNKS[k][2], 1, SCATTER_NEARER)) for k, out in enumerate(outgoing)]
    sums = call(
        functools.partial(keep_kernel, third),
        [vmem(value) for value in (*parts[3:], weights[0], weights[1])],
        [("vmem", (rows // 2, third), jnp.float32)] * 3,
        flops=2 * rows * local_ff * half,
        megabytes=8,
    )

    for stage in (2, 1, 0):
        sums = [value + new.astype(jnp.float32) for value, new in zip(sums, received)]
        if stage:
            cut = sums[0].shape[0] // 2
            received = [
                send(value[cut:].astype(jnp.bfloat16), neighbour(CHUNKS[k][stage - 1], 1, SCATTER_NEARER))
                for k, value in enumerate(sums)
            ]
            sums = [value[:cut] for value in sums]
    value = jnp.concatenate(sums, axis=1)
    cut = value.shape[0] // 2
    leaving, parts = lax.optimization_barrier((value[cut:].astype(jnp.bfloat16), parts))
    arriving = send(leaving, neighbour("z", 0, SCATTER_NEARER))
    grads = call(
        functools.partial(weight_kernel, third),
        [vmem(piece) for k in range(3) for piece in (held[k], last[k])]
        + [vmem(value) for value in parts[:3]],
        [("hbm", (local_ff, half), jnp.bfloat16)] * 3,
        [pltpu.VMEM((3, local_ff, half), jnp.bfloat16), pltpu.SemaphoreType.DMA((9,))],
        limit=24,
        flops=6 * rows * local_ff * half,
        megabytes=24,
    )
    arriving, (gate_grad, up_grad, down_grad) = lax.optimization_barrier((arriving, grads))
    value = value[:cut] + arriving.astype(jnp.float32)
    cut = value.shape[0] // 4
    value = value[:cut] + sum(
        send(value[i * cut : (i + 1) * cut].astype(jnp.bfloat16), neighbour(axes, 0, SCATTER_NEARER)).astype(
            jnp.float32
        )
        for i, axes in ((1, "x"), (2, "y"), (3, "xy"))
    )
    value = value.astype(jnp.bfloat16)
    mine = jnp.where(core == 0, value[:micro], value[micro:])
    theirs = send(jnp.where(core == 0, value[micro:], value[:micro]), OTHER_CORE)
    input_grad = jnp.concatenate(
        [jnp.where(core == 0, mine, theirs), jnp.where(core == 0, theirs, mine)], axis=1
    )[:, None, :]
    return input_grad, gate_grad, up_grad, down_grad


def solution(mesh):
    return jax.shard_map(
        shards,
        mesh=mesh,
        in_specs=(
            P(None, ("rep", "tp", "att"), None),
            P(None, ("rep", "tp", "att"), None),
            P(("tp", "att"), None),
            P(("tp", "att"), None),
            P(("tp", "att"), None),
        ),
        out_specs=(
            P(None, ("rep", "tp", "att"), None),
            P(("tp", "att"), "rep"),
            P(("tp", "att"), "rep"),
            P(("tp", "att"), "rep"),
        ),
        check_vma=False,
    )
```
